32 devices in a mesh: group: 8 (over z, core), replica: 4 (over y, x).
Axes of the slice: x: 2, y: 2, z: 4, core: 2. Of those that a mesh axis runs over, the one named last changes fastest.
Arguments:
- tokens: bfloat16 [32, 1024, 768], P(('group', 'replica')), may hold values from -6 to 6
- segments: int32 [32, 1024], P(('group', 'replica')), may hold values from 0 to 2, as said below
- norm_gain: bfloat16 [768], P('group'), may hold values from 0.5 to 1.5
- in_weight: bfloat16 [768, 3352], P('group'), may hold values from -0.21875 to 0.21875
- conv_weight: bfloat16 [4, 1792], P(None, 'group'), may hold values from -3 to 3
- conv_bias: bfloat16 [1792], P('group'), may hold values from -3 to 3
- step_bias: float32 [24], replicated, may hold values from -4 to -1
- log_decay: float32 [24], replicated, may hold values from -2 to 2
- skip_scale: float32 [24], replicated, may hold values from 0.5 to 2
- out_gain: bfloat16 [1536], P('group'), may hold values from 0.5 to 1.5
- out_weight: bfloat16 [1536, 768], P('group'), may hold values from -0.15625 to 0.15625
- cotangent: bfloat16 [32, 1024, 768], P(('group', 'replica')), may hold values from -6 to 6
Outputs:
- layer_out: bfloat16 [32, 1024, 768], P(('group', 'replica'))
- input_grad: bfloat16 [32, 1024, 768], P(('group', 'replica'))
- grad_norm_gain: float32 [768], P('group')
- grad_in_weight: float32 [768, 3352], P('group')
- grad_conv_weight: float32 [4, 1792], P(None, 'group')
- grad_conv_bias: float32 [1792], P('group')
- grad_step_bias: float32 [24], replicated
- grad_log_decay: float32 [24], replicated
- grad_skip_scale: float32 [24], replicated
- grad_out_gain: float32 [1536], P('group')
- grad_out_weight: float32 [1536, 768], P('group')
The draws below stay inside these ranges and needn't reach their ends.
Inputs may be any that keep to these rules, and one draw needn't show every extreme that they name: `segments`: within each sequence the segment numbers are 0, 1, 2 in runs that never fall: three documents, each of 200 tokens or more.
All inputs are finite; a program needn't handle non-finite values.
Results may differ from the reference program's by a relative error of at most 0.015.
Values may be sent and summed in bfloat16 or wider, within the bound.
A program may use at most 256 MiB of HBM per device.

```python
import math
import jax
import jax.numpy as jnp
from jax import lax

D = 768
HEADS = 24
CONV = 4
STRETCH = 256
SEQ_LEN = 1024
INNER = 1536
XBC = 1792
PROJ = 3352
SEQS = 32


def draw_segments(key, part):
    key = jax.random.fold_in(key, 11)
    floor_len = SEQ_LEN * 200 // 1024
    first_key, second_key = jax.random.split(key)
    first_cut = jax.random.randint(first_key, (SEQS, 1), floor_len, SEQ_LEN - 2 * floor_len + 1)
    span_hi = SEQ_LEN - floor_len - first_cut + 1
    offsets = jax.random.randint(second_key, (SEQS, 1), 0, 1 << 20)
    second_cut = first_cut + floor_len + offsets % (span_hi - floor_len)
    positions = jnp.arange(SEQ_LEN, dtype=jnp.int32)[None, :]
    return ((positions >= first_cut).astype(jnp.int32) + (positions >= second_cut).astype(jnp.int32)).astype(jnp.int32)


def block_levels(rng, extent, shards, smallest, top_value):
    def one(axis_at, parts):
        draws = jax.random.uniform(jax.random.fold_in(jax.random.fold_in(rng, 6), axis_at), (parts,), jnp.float32, smallest / len(shards), top_value / len(shards))
        return jnp.repeat(jnp.exp(draws), extent[axis_at] // parts).reshape((-1,) + (1,) * (len(extent) - axis_at - 1))

    factor_of = one(*shards[0])
    for cut in shards[1:]:
        factor_of = factor_of * one(*cut)
    return factor_of


def bell_draw(key, dims, width, most, cuts=(), kind=jnp.bfloat16):
    values = width * jax.random.normal(key, dims, jnp.float32)
    if cuts:
        values = values * block_levels(key, dims, cuts, -0.22, 0.18)
    return jnp.clip(values, -most, most).astype(kind)


def setup_inputs(seed: int = 0) -> dict:
    key_of = jax.random.split(jax.random.key(seed), 13)
    return {
        "tokens": bell_draw(key_of[0], (SEQS, SEQ_LEN, D), 1.0, 6.0, ((0, 32),)),
        "segments": draw_segments(jax.random.fold_in(key_of[12], 71), 0),
        "norm_gain": jnp.clip(1.0 + 0.1 * jax.random.normal(key_of[2], (D,), jnp.float32), 0.5, 1.5).astype(jnp.bfloat16),
        "in_weight": bell_draw(key_of[3], (D, PROJ), D ** -0.5, 0.21875, ((0, 8),)),
        "conv_weight": bell_draw(key_of[4], (CONV, XBC), CONV ** -0.5, 3.0, ((1, 8),)),
        "conv_bias": bell_draw(key_of[5], (XBC,), 0.5, 3.0, ((0, 8),)),
        "step_bias": jnp.clip(jax.random.uniform(key_of[6], (HEADS,), jnp.float32, -4.0, -1.0), -4.0, -1.0),
        "log_decay": jnp.clip(jax.random.uniform(key_of[7], (HEADS,), jnp.float32, -2.0, 2.0), -2.0, 2.0),
        "skip_scale": jnp.clip(jax.random.uniform(key_of[8], (HEADS,), jnp.float32, 0.5, 2.0), 0.5, 2.0),
        "out_gain": jnp.clip(1.0 + 0.1 * jax.random.normal(key_of[9], (INNER,), jnp.float32), 0.5, 1.5).astype(jnp.bfloat16),
        "out_weight": bell_draw(key_of[10], (INNER, D), INNER ** -0.5, 0.15625, ((0, 8),)),
        "cotangent": bell_draw(key_of[11], (SEQS, SEQ_LEN, D), 1.0, 6.0, ((0, 32),)),
    }


highest_precision = lax.Precision.HIGHEST

@jax.custom_vjp
def low(v):
    return lax.optimization_barrier(v.astype(jnp.bfloat16)).astype(jnp.float32)

@jax.custom_vjp
def reduced_backward(v):
    return v

def low_keep(v):
    return (low(v), None)

def low_pass(kept, grad):
    return (grad,)

def back_keep(v):
    return (v, None)

def back_low(kept, grad):
    return (low(grad),)
low.defvjp(low_keep, low_pass)
reduced_backward.defvjp(back_keep, back_low)

def rms_scale(values, gain):
    return values * lax.rsqrt(lax.optimization_barrier(jnp.mean(values * values, axis=-1, keepdims=True)) + 1e-05) * gain

def conv_silu(columns, segment, kernel, offsets):
    kernel_len = kernel.shape[0]
    summed = offsets[None, :] + kernel[kernel_len - 1][None, :] * columns
    for offset in range(1, kernel_len):
        earlier = jnp.concatenate([jnp.zeros((offset, columns.shape[1]), jnp.float32), columns[:-offset]], axis=0)
        earlier_seg = jnp.concatenate([jnp.full((offset,), -1, jnp.int32), segment[:-offset]])
        kept_mask = (earlier_seg == segment).astype(jnp.float32)
        summed = summed + kernel[kernel_len - 1 - offset][None, :] * earlier * kept_mask[:, None]
    return jax.nn.silu(summed)

def block_step(running_state, inputs):
    state, last_seg = running_state
    values, in_basis, out_basis, step_size, cumulative, segment = inputs
    positions = jnp.arange(segment.shape[0])
    causal = positions[:, None] >= positions[None, :]
    same_doc = segment[:, None] == segment[None, :]
    masked = (causal & same_doc)[:, :, None]
    spread = cumulative[:, None, :] - cumulative[None, :, :]
    decays = jnp.where(masked, jnp.exp(jnp.where(masked, spread, 0.0)), 0.0)
    intersection = jnp.dot(out_basis, in_basis.T, precision=highest_precision)
    mixing = intersection[:, :, None] * decays * step_size[None, :, :]
    within = jnp.einsum('ijh,jhp->ihp', mixing, values, precision=highest_precision)
    carried = (segment == last_seg).astype(jnp.float32)
    from_state = jnp.einsum('in,hpn->ihp', out_basis, state, precision=highest_precision)
    from_state = from_state * (jnp.exp(cumulative) * carried[:, None])[:, :, None]
    tail_same = (segment == segment[-1]).astype(jnp.float32)
    to_end = jnp.exp(cumulative[-1][None, :] - cumulative) * step_size * tail_same[:, None]
    keep_old = jnp.exp(cumulative[-1]) * (segment[-1] == last_seg).astype(jnp.float32)
    new_state = state * keep_old[:, None, None] + jnp.einsum('jh,jhp,jn->hpn', to_end, values, in_basis, precision=highest_precision)
    return ((new_state, segment[-1]), within + from_state)

def mixer_sequence(projected_rows, segment, kernel, offsets, dt_shift, decay_param, skip_param, gain_param):
    length_all = projected_rows.shape[0]
    inner_width = gain_param.shape[0]
    head_count = dt_shift.shape[0]
    state_size = (projected_rows.shape[1] - 2 * inner_width - head_count) // 2
    gate_part = projected_rows[:, :inner_width]
    conv_out = conv_silu(projected_rows[:, inner_width:2 * inner_width + 2 * state_size], segment, kernel, offsets)
    values = conv_out[:, :inner_width].reshape(length_all, head_count, inner_width // head_count)
    in_basis = conv_out[:, inner_width:inner_width + state_size]
    out_basis = conv_out[:, inner_width + state_size:]
    step_size = jax.nn.softplus(projected_rows[:, 2 * inner_width + 2 * state_size:] + dt_shift)
    decay_rates = -jnp.exp(decay_param)
    blocks = length_all // STRETCH
    cumulative = jnp.cumsum((step_size * decay_rates).reshape(blocks, STRETCH, head_count), axis=1)
    inputs = (values.reshape(blocks, STRETCH, head_count, -1), in_basis.reshape(blocks, STRETCH, -1), out_basis.reshape(blocks, STRETCH, -1), step_size.reshape(blocks, STRETCH, head_count), cumulative, segment.reshape(blocks, STRETCH))
    initial = (jnp.zeros((head_count, inner_width // head_count, state_size), jnp.float32), jnp.array(-1, jnp.int32))
    final_state, outputs = lax.scan(jax.checkpoint(block_step), initial, inputs)
    scanned = outputs.reshape(length_all, head_count, -1) + skip_param[None, :, None] * values
    gated = scanned.reshape(length_all, inner_width) * jax.nn.silu(gate_part)
    return rms_scale(gated, gain_param)

def mix_all(projected_rows, segments, kernel, offsets, dt_shift, decay_param, skip_param, gain_param):

    def per_sequence(block_pair):
        return mixer_sequence(block_pair[0], block_pair[1], kernel, offsets, dt_shift, decay_param, skip_param, gain_param)
    return lax.map(jax.checkpoint(per_sequence), (projected_rows, segments))

def reference(tokens, segments, norm_gain, in_weight, conv_weight, conv_bias, step_bias, log_decay, skip_scale, out_gain, out_weight, cotangent):
    per_block = math.gcd(SEQS, max(1, 4096 // SEQ_LEN))
    block_count = SEQS // per_block
    seg_blocks = segments.reshape(block_count, per_block, SEQ_LEN)

    def forward(tokens_f, gain_in, input_weight, kernel, offsets, dt_shift, decay_param, skip_param, gain_out, output_weight):

        def block_fn(running_state, block_pair):
            tokens_per_block, block_segs = block_pair
            normalized_input = low(rms_scale(tokens_per_block, gain_in))
            projected_rows = reduced_backward(jnp.einsum('ryj,jb->ryb', normalized_input, input_weight, precision=highest_precision))
            mixer_output = low(mix_all(projected_rows, block_segs, kernel, offsets, dt_shift, decay_param, skip_param, gain_out))
            return (running_state, tokens_per_block + jnp.einsum('vrx,xw->vrw', mixer_output, output_weight, precision=highest_precision))
        blocks_in = tokens_f.reshape(block_count, per_block, SEQ_LEN, -1)
        unused, results = lax.scan(jax.checkpoint(block_fn), jnp.zeros((), jnp.float32), (blocks_in, seg_blocks))
        return results.reshape(tokens_f.shape)
    outputs, pullback = jax.vjp(forward, tokens.astype(jnp.float32), norm_gain.astype(jnp.float32), in_weight.astype(jnp.float32), conv_weight.astype(jnp.float32), conv_bias.astype(jnp.float32), step_bias, log_decay, skip_scale, out_gain.astype(jnp.float32), out_weight.astype(jnp.float32))
    grads = pullback(cotangent.astype(jnp.float32))
    return (outputs.astype(jnp.bfloat16), grads[0].astype(jnp.bfloat16), grads[1], grads[2], grads[3], grads[4], grads[5], grads[6], grads[7], grads[8], grads[9])
```

```python
import functools

import jax
import jax.numpy as jnp
from jax import lax
from jax.experimental import pallas as pl
from jax.experimental.pallas import tpu as pltpu
from jax.sharding import PartitionSpec as P

Q = 128
LANES = 128
FAR = -1e30
HIGHEST = lax.Precision.HIGHEST
F32 = jnp.float32
BF16 = jnp.bfloat16


def dot_nn(a, b, precision=None):
    return lax.dot_general(
        a, b, (((1,), (0,)), ((), ())), preferred_element_type=F32, precision=precision
    )


def dot_nt(a, b, precision=None):
    return lax.dot_general(
        a, b, (((1,), (1,)), ((), ())), preferred_element_type=F32, precision=precision
    )


def dot_tn(a, b):
    return lax.dot_general(a, b, (((0,), (0,)), ((), ())), preferred_element_type=F32)


def sigmoid(v):
    return 1.0 / (1.0 + jnp.exp(-v))


def softplus(v):
    return jnp.maximum(v, 0.0) + jnp.log(1.0 + jnp.exp(-jnp.abs(v)))


def grid_iotas():
    rows = lax.broadcasted_iota(jnp.int32, (Q, Q), 0)
    cols = lax.broadcasted_iota(jnp.int32, (Q, Q), 1)
    return rows, cols


def spread_pair(table, pair, left):
    a = jnp.broadcast_to(table[:, 2 * pair : 2 * pair + 1], (Q, LANES))
    b = jnp.broadcast_to(table[:, 2 * pair + 1 : 2 * pair + 2], (Q, LANES))
    return a, b, jnp.where(left, a, b)


def halves(v, left):
    zero = jnp.zeros_like(v)
    return jnp.concatenate([jnp.where(left, v, zero), jnp.where(left, zero, v)], axis=0)


def forward_kernel(
    inner, proj, segc, segr, taps, heads, wide,
    pre_o, y_o, state_o, cum_o, mixed_o,
    state, cbuf, sbuf, conv, gated_s,
):
    pairs = inner // LANES
    xbc = conv.shape[1]

    @pl.when(pl.program_id(1) == 0)
    def _():
        state[...] = jnp.zeros_like(state)
        cbuf[0:8, :] = jnp.zeros((8, xbc), F32)
        sbuf[0:8, :] = jnp.full((8, LANES), -1.0, F32)

    seg = segc[...]
    sbuf[8 : 8 + Q, :] = seg
    cbuf[8 : 8 + Q, :] = proj[:, inner : inner + xbc]
    masks = [None] + [(sbuf[8 - k : 8 - k + Q, :] == seg).astype(F32) for k in (1, 2, 3)]
    for g in range(xbc // LANES):
        cs = slice(g * LANES, (g + 1) * LANES)
        acc = taps[4:5, cs] + taps[3:4, cs] * cbuf[8 : 8 + Q, cs]
        for k in (1, 2, 3):
            acc = acc + taps[3 - k : 4 - k, cs] * (cbuf[8 - k : 8 - k + Q, cs] * masks[k])
        pre_o[:, cs] = acc
        conv[:, cs] = acc * sigmoid(acc)
    rows, cols = grid_iotas()
    left = cols < 64
    dt = softplus(proj[:, inner + xbc : inner + xbc + LANES] + heads[0:1, :])
    cum = dot_nn((rows >= cols).astype(F32), dt * heads[1:2, :], HIGHEST)
    cum_o[...] = cum
    cum_t = cum.T
    b_low = conv[:, inner : inner + LANES].astype(BF16)
    c_low = conv[:, inner + LANES : inner + 2 * LANES].astype(BF16)
    inter = dot_nt(c_low, b_low)
    bias = jnp.where((rows >= cols) & (seg == segr[0, 0:1, :]), 0.0, FAR)
    last_seg = sbuf[7:8, :]
    end_seg = sbuf[7 + Q : 8 + Q, :]
    carried = (seg == last_seg).astype(F32)
    tail = (seg == end_seg).astype(F32)
    keep = (end_seg == last_seg).astype(F32)
    squares = jnp.zeros((Q, LANES), F32)
    for p in range(pairs):
        cs = slice(p * LANES, (p + 1) * LANES)
        cum_a, cum_b, cum_p = spread_pair(cum, p, left)
        _, _, dt_p = spread_pair(dt, p, left)
        mix_a = (inter * jnp.exp(cum_a - cum_t[2 * p : 2 * p + 1, :] + bias)).astype(BF16)
        mix_b = (inter * jnp.exp(cum_b - cum_t[2 * p + 1 : 2 * p + 2, :] + bias)).astype(BF16)
        x = conv[:, cs]
        xd = (dt_p * x).astype(BF16)
        y = dot_nn(jnp.concatenate([mix_a, mix_b], axis=1), halves(xd, left))
        old = state[:, cs]
        old_low = old.astype(BF16)
        state_o[0, :, cs] = old_low
        y = y + jnp.exp(cum_p) * carried * dot_nn(c_low, old_low)
        y_o[:, cs] = y
        end = cum_p[Q - 1 : Q, :]
        xe = (jnp.exp(end - cum_p) * tail * xd.astype(F32)).astype(BF16)
        state[:, cs] = old * (jnp.exp(end) * keep) + dot_tn(b_low, xe)
        gate = proj[:, cs]
        gated = (y + wide[0:1, cs] * x) * (gate * sigmoid(gate))
        gated_s[:, cs] = gated
        squares = squares + gated * gated
    r = lax.rsqrt(jnp.sum(squares, axis=1, keepdims=True) / inner + 1e-5)
    r = jnp.broadcast_to(r, (Q, LANES))
    for p in range(pairs):
        cs = slice(p * LANES, (p + 1) * LANES)
        mixed_o[:, cs] = (gated_s[:, cs] * r * wide[1:2, cs]).astype(BF16)
    cbuf[0:8, :] = cbuf[Q : Q + 8, :]
    sbuf[0:8, :] = sbuf[Q : Q + 8, :]


def backward_kernel(
    inner, proj, pre, y_i, state_i, cum_i, dmix, segc, segr, segp, taps, heads, wide, pick,
    gproj_o, gtaps_o, gwide_o, gheads_o,
    dstate, dbuf, sbuf, conv, slope, dcum_s, ddt_s, far_s, held_s,
):
    pairs = inner // LANES
    xbc = conv.shape[1]

    @pl.when(pl.program_id(1) == 0)
    def _():
        dstate[...] = jnp.zeros_like(dstate)
        dbuf[Q : Q + 8, :] = jnp.zeros((8, xbc), F32)
        sbuf[Q : Q + 8, :] = jnp.full((8, LANES), -1.0, F32)

    @pl.when((pl.program_id(0) == 0) & (pl.program_id(1) == 0))
    def _():
        gtaps_o[...] = jnp.zeros_like(gtaps_o)
        gwide_o[...] = jnp.zeros_like(gwide_o)
        gheads_o[...] = jnp.zeros_like(gheads_o)

    seg = segc[...]
    sbuf[0:Q, :] = seg
    rows, cols = grid_iotas()
    left = cols < 64
    for g in range(xbc // LANES):
        cs = slice(g * LANES, (g + 1) * LANES)
        v = pre[:, cs]
        s = sigmoid(v)
        conv[:, cs] = v * s
        slope[:, cs] = s * (1.0 + v * (1.0 - s))
    squares = jnp.zeros((Q, LANES), F32)
    along = jnp.zeros((Q, LANES), F32)
    for p in range(pairs):
        cs = slice(p * LANES, (p + 1) * LANES)
        gate = proj[:, cs]
        gated = (y_i[:, cs] + wide[0:1, cs] * conv[:, cs]) * (gate * sigmoid(gate))
        squares = squares + gated * gated
        along = along + dmix[:, cs] * wide[1:2, cs] * gated
    r = lax.rsqrt(jnp.sum(squares, axis=1, keepdims=True) / inner + 1e-5)
    lean = jnp.sum(along, axis=1, keepdims=True) / inner * r * r
    r = jnp.broadcast_to(r, (Q, LANES))
    lean = jnp.broadcast_to(lean, (Q, LANES))

    raw = proj[:, inner + xbc : inner + xbc + LANES] + heads[0:1, :]
    dt = softplus(raw)
    cum = cum_i[...]
    cum_t = cum.T
    b_low = conv[:, inner : inner + LANES].astype(BF16)
    c_low = conv[:, inner + LANES : inner + 2 * LANES].astype(BF16)
    inter_t = dot_nt(b_low, c_low)
    bias_t = jnp.where((rows <= cols) & (seg == segr[0, 0:1, :]), 0.0, FAR)
    last_seg = segp[0, 0:1, :]
    end_seg = sbuf[Q - 1 : Q, :]
    carried = (seg == last_seg).astype(F32)
    tail = (seg == end_seg).astype(F32)
    keep = (end_seg == last_seg).astype(F32)
    dinter_t = jnp.zeros((Q, Q), F32)
    d_b = jnp.zeros((Q, LANES), F32)
    d_c = jnp.zeros((Q, LANES), F32)
    for p in range(pairs):
        cs = slice(p * LANES, (p + 1) * LANES)
        x = conv[:, cs]
        y = y_i[:, cs]
        gate = proj[:, cs]
        sg = sigmoid(gate)
        scanned = y + wide[0:1, cs] * x
        silu_gate = gate * sg
        gated = scanned * silu_gate
        dm = dmix[:, cs]
        gwide_o[1:2, cs] += jnp.sum(dm * gated * r, axis=0, keepdims=True)
        dgated = r * (dm * wide[1:2, cs] - gated * lean)
        gproj_o[:, cs] = (dgated * scanned * (sg * (1.0 + gate * (1.0 - sg)))).astype(BF16)
        dscan = dgated * silu_gate
        gwide_o[0:1, cs] += jnp.sum(dscan * x, axis=0, keepdims=True)

        cum_a, cum_b, cum_p = spread_pair(cum, p, left)
        _, _, dt_p = spread_pair(dt, p, left)
        decay_a = jnp.exp(cum_t[2 * p : 2 * p + 1, :] - cum_a + bias_t)
        decay_b = jnp.exp(cum_t[2 * p + 1 : 2 * p + 2, :] - cum_b + bias_t)
        mix_a = (inter_t * decay_a).astype(BF16)
        mix_b = (inter_t * decay_b).astype(BF16)
        dy = dscan.astype(BF16)
        dy_wide = dy.astype(F32)
        xd = (dt_p * x).astype(BF16)
        xd_wide = xd.astype(F32)
        end = cum_p[Q - 1 : Q, :]
        to_end = jnp.exp(end - cum_p) * tail
        dst = dstate[:, cs]
        dst_low = dst.astype(BF16)
        dxd = dot_nn(jnp.concatenate([mix_a, mix_b], axis=1), halves(dy, left))
        dxd_far = to_end * dot_nn(b_low, dst_low)
        dcum_s[:, cs] = dy_wide * y - xd_wide * dxd
        far_s[:, cs] = xd_wide * dxd_far
        dxd = dxd + dxd_far
        dmix_t = dot_nt(halves(xd, left), dy)
        dinter_t = dinter_t + dmix_t[0:Q, :] * decay_a + dmix_t[Q : 2 * Q, :] * decay_b
        edy = (jnp.exp(cum_p) * carried * dy_wide).astype(BF16)
        xe = (to_end * xd_wide).astype(BF16)
        d_b = d_b + dot_nt(xe, dst_low)
        d_c = d_c + dot_nt(edy, state_i[0, :, cs])
        kept = dst * (jnp.exp(end) * keep)
        held = jnp.sum(kept * state_i[0, :, cs].astype(F32), axis=0, keepdims=True)
        held_s[:, cs] = jnp.broadcast_to(held, (8, LANES))
        dstate[:, cs] = kept + dot_tn(c_low, edy)
        ddt_s[:, cs] = x * dxd
        dbuf[0:Q, cs] = (dscan * wide[0:1, cs] + dt_p * dxd) * slope[:, cs]
    d_b = d_b + dot_nn(dinter_t.astype(BF16), c_low)
    d_c = d_c + dot_nn(dinter_t.T.astype(BF16), b_low)
    bs = slice(inner, inner + LANES)
    os = slice(inner + LANES, inner + 2 * LANES)
    dbuf[0:Q, bs] = d_b * slope[:, bs]
    dbuf[0:Q, os] = d_c * slope[:, os]

    dcum = dot_nn(dcum_s[...], pick[...], HIGHEST)
    ddt = dot_nn(ddt_s[...], pick[...], HIGHEST)
    rate = heads[1:2, :]
    far = dot_nn(far_s[...], pick[...], HIGHEST)
    held = dot_nn(held_s[...], pick[...], HIGHEST)[0:1, :]
    later = dot_nn((rows <= cols).astype(F32), dcum, HIGHEST)
    later = later + dot_nn((rows > cols).astype(F32), far, HIGHEST) + held
    gheads_o[1:2, :] += jnp.sum(later * dt * rate, axis=0, keepdims=True)
    dstep = (ddt + later * rate) * sigmoid(raw)
    gheads_o[0:1, :] += jnp.sum(dstep, axis=0, keepdims=True)
    gproj_o[:, inner + xbc : inner + xbc + LANES] = dstep.astype(BF16)

    masks = [None] + [(sbuf[k : k + Q, :] == seg).astype(F32) for k in (1, 2, 3)]
    for g in range(xbc // LANES):
        cs = slice(g * LANES, (g + 1) * LANES)
        here = proj[:, inner + g * LANES : inner + (g + 1) * LANES]
        now = dbuf[0:Q, cs]
        total = taps[3:4, cs] * now
        gtaps_o[4:5, cs] += jnp.sum(now, axis=0, keepdims=True)
        gtaps_o[3:4, cs] += jnp.sum(now * here, axis=0, keepdims=True)
        for k in (1, 2, 3):
            moved = dbuf[k : k + Q, cs] * masks[k]
            total = total + taps[3 - k : 4 - k, cs] * moved
            gtaps_o[3 - k : 4 - k, cs] += jnp.sum(moved * here, axis=0, keepdims=True)
        gproj_o[:, inner + g * LANES : inner + (g + 1) * LANES] = total.astype(BF16)
    dbuf[Q : Q + 8, :] = dbuf[0:8, :]
    sbuf[Q : Q + 8, :] = sbuf[0:8, :]


VMEM_LIMIT = 52 * 1024 * 1024


def mixer_tables(segments, taps, bias, step_bias, log_decay, skip_scale, gain):
    seqs, length = segments.shape
    chunks = length // Q
    heads, inner = step_bias.shape[0], gain.shape[0]
    segf = segments.astype(F32)
    segc = jnp.broadcast_to(segf.reshape(seqs * length, 1), (seqs * length, LANES))
    blocks = segf.reshape(seqs * chunks, 1, Q)
    segr = jnp.broadcast_to(blocks, (seqs * chunks, 8, Q))
    lasts = segf.reshape(seqs, chunks, Q)[:, :, Q - 1]
    before = jnp.concatenate([jnp.full((seqs, 1), -1.0, F32), lasts[:, :-1]], axis=1)
    segp = jnp.broadcast_to(before.reshape(seqs * chunks, 1, 1), (seqs * chunks, 8, LANES))
    taps8 = jnp.concatenate([taps, bias[None], jnp.zeros((3, taps.shape[1]), F32)], axis=0)
    head8 = jnp.zeros((8, LANES), F32)
    head8 = head8.at[0, :heads].set(step_bias).at[1, :heads].set(-jnp.exp(log_decay))
    wide8 = jnp.concatenate(
        [jnp.repeat(skip_scale, inner // heads)[None], gain[None], jnp.zeros((6, inner), F32)], axis=0
    )
    owner = jnp.arange(inner)[:, None] // (inner // heads)
    pick = (owner == jnp.arange(LANES)[None, :]).astype(F32)
    return segc, segr, segp, taps8, head8, wide8, pick


def mixer_forward(proj, tables, seqs):
    segc, segr, segp, taps8, head8, wide8, pick = tables
    rows, width = proj.shape
    inner, xbc = wide8.shape[1], taps8.shape[1]
    chunks = rows // seqs // Q

    def at(s, c):
        return (s * chunks + c, 0)

    def at3(s, c):
        return (s * chunks + c, 0, 0)

    def still(s, c):
        return (0, 0)

    return pl.pallas_call(
        functools.partial(forward_kernel, inner),
        grid=(seqs, chunks),
        in_specs=[
            pl.BlockSpec((Q, width), at),
            pl.BlockSpec((Q, LANES), at),
            pl.BlockSpec((1, 8, Q), at3),
            pl.BlockSpec((8, xbc), still),
            pl.BlockSpec((8, LANES), still),
            pl.BlockSpec((8, inner), still),
        ],
        out_specs=[
            pl.BlockSpec((Q, xbc), at),
            pl.BlockSpec((Q, inner), at),
            pl.BlockSpec((1, LANES, inner), at3),
            pl.BlockSpec((Q, LANES), at),
            pl.BlockSpec((Q, inner), at),
        ],
        out_shape=[
            jax.ShapeDtypeStruct((rows, xbc), F32),
            jax.ShapeDtypeStruct((rows, inner), F32),
            jax.ShapeDtypeStruct((seqs * chunks, LANES, inner), BF16),
            jax.ShapeDtypeStruct((rows, LANES), F32),
            jax.ShapeDtypeStruct((rows, inner), BF16),
        ],
        scratch_shapes=[
            pltpu.VMEM((LANES, inner), F32),
            pltpu.VMEM((Q + 8, xbc), F32),
            pltpu.VMEM((Q + 8, LANES), F32),
            pltpu.VMEM((Q, xbc), F32),
            pltpu.VMEM((Q, inner), F32),
        ],
        compiler_params=pltpu.CompilerParams(vmem_limit_bytes=VMEM_LIMIT),
        cost_estimate=pl.CostEstimate(flops=2 * 10**9, bytes_accessed=10**8, transcendentals=10**7),
        name="mixer_forward",
    )(proj, segc, segr, taps8, head8, wide8)


def mixer_backward(proj, pre, y, states, cum, dmix, tables, seqs):
    segc, segr, segp, taps8, head8, wide8, pick = tables
    rows, width = proj.shape
    inner, xbc = wide8.shape[1], taps8.shape[1]
    chunks = rows // seqs // Q

    def at(s, c):
        return (s * chunks + chunks - 1 - c, 0)

    def at3(s, c):
        return (s * chunks + chunks - 1 - c, 0, 0)

    def still(s, c):
        return (0, 0)

    return pl.pallas_call(
        functools.partial(backward_kernel, inner),
        grid=(seqs, chunks),
        in_specs=[
            pl.BlockSpec((Q, width), at),
            pl.BlockSpec((Q, xbc), at),
            pl.BlockSpec((Q, inner), at),
            pl.BlockSpec((1, LANES, inner), at3),
            pl.BlockSpec((Q, LANES), at),
            pl.BlockSpec((Q, inner), at),
            pl.BlockSpec((Q, LANES), at),
            pl.BlockSpec((1, 8, Q), at3),
            pl.BlockSpec((1, 8, LANES), at3),
            pl.BlockSpec((8, xbc), still),
            pl.BlockSpec((8, LANES), still),
            pl.BlockSpec((8, inner), still),
            pl.BlockSpec((inner, LANES), still),
        ],
        out_specs=[
            pl.BlockSpec((Q, width), at),
            pl.BlockSpec((8, xbc), still),
            pl.BlockSpec((8, inner), still),
            pl.BlockSpec((8, LANES), still),
        ],
        out_shape=[
            jax.ShapeDtypeStruct((rows, width), BF16),
            jax.ShapeDtypeStruct((8, xbc), F32),
            jax.ShapeDtypeStruct((8, inner), F32),
            jax.ShapeDtypeStruct((8, LANES), F32),
        ],
        scratch_shapes=[
            pltpu.VMEM((LANES, inner), F32),
            pltpu.VMEM((Q + 8, xbc), F32),
            pltpu.VMEM((Q + 8, LANES), F32),
            pltpu.VMEM((Q, xbc), F32),
            pltpu.VMEM((Q, xbc), F32),
            pltpu.VMEM((Q, inner), F32),
            pltpu.VMEM((Q, inner), F32),
            pltpu.VMEM((Q, inner), F32),
            pltpu.VMEM((8, inner), F32),
        ],
        compiler_params=pltpu.CompilerParams(vmem_limit_bytes=VMEM_LIMIT),
        cost_estimate=pl.CostEstimate(
            flops=5 * 10**9, bytes_accessed=2 * 10**8, transcendentals=2 * 10**7
        ),
        name="mixer_backward",
    )(proj, pre, y, states, cum, dmix, segc, segr, segp, taps8, head8, wide8, pick)


def pad_to(v, size):
    return jnp.concatenate([v, jnp.zeros((size - v.shape[0],), v.dtype)])


def per_device(
    tokens, segments, norm_gain, in_weight, conv_weight, conv_bias, step_bias, log_decay,
    skip_scale, out_gain, out_weight, cotangent,
):
    seqs, length, model = tokens.shape
    rows = seqs * length
    heads = step_bias.shape[0]
    proj_width = in_weight.shape[1]
    full_width = -(-proj_width // LANES) * LANES
    n_norm, n_conv, n_out = norm_gain.shape[0], conv_bias.shape[0], out_gain.shape[0]

    padded = jnp.pad(in_weight, ((0, 0), (0, full_width - proj_width)))
    small = jnp.concatenate([norm_gain, conv_weight.reshape(-1), conv_bias, out_gain])
    n_small = small.shape[0]
    small_rows = -(-n_small // 2048) * 16
    small = pad_to(small, small_rows * LANES).reshape(small_rows, LANES)
    small = lax.all_gather(small, "group", axis=0, tiled=True)
    full_in = lax.all_gather(padded, "group", axis=0, tiled=True)
    full_out = lax.all_gather(out_weight, "group", axis=0, tiled=True)
    small = small.reshape(-1, small_rows * LANES).astype(F32)
    shards = small.shape[0]
    cuts = [n_norm, n_norm + 4 * n_conv, n_norm + 5 * n_conv, n_small]
    gain_in = small[:, : cuts[0]].reshape(-1)
    taps = small[:, cuts[0] : cuts[1]].reshape(shards, 4, n_conv)
    taps = taps.transpose(1, 0, 2).reshape(4, -1)
    bias = small[:, cuts[1] : cuts[2]].reshape(-1)
    gain_out = small[:, cuts[2] : cuts[3]].reshape(-1)
    tables = mixer_tables(segments, taps, bias, step_bias, log_decay, skip_scale, gain_out)
    inner = gain_out.shape[0]

    flat = tokens.reshape(rows, model).astype(F32)
    r = lax.rsqrt(jnp.mean(flat * flat, axis=-1, keepdims=True) + 1e-05)
    normed = (flat * r * gain_in).astype(BF16)
    cot = cotangent.reshape(rows, model)
    proj = jnp.dot(normed, full_in, preferred_element_type=F32)
    pre, y, states, cum, mixed = mixer_forward(proj, tables, seqs)
    grad_out = dot_tn(mixed, cot).astype(BF16)
    grad_mixed = dot_nt(cot, full_out)
    grad_out = lax.psum_scatter(grad_out, "group", scatter_dimension=0, tiled=True)
    grad_out = lax.all_gather(grad_out, "replica", axis=0, tiled=False)
    grad_out = jnp.sum(grad_out.astype(F32), axis=0)
    branch = dot_nn(mixed, full_out)
    layer_out = (flat + branch).astype(BF16).reshape(tokens.shape)
    gproj, gtaps, gwide, gheads = mixer_backward(
        proj, pre, y, states, cum, grad_mixed, tables, seqs
    )
    grad_in = dot_tn(normed, gproj).astype(BF16)
    grad_in = lax.psum_scatter(grad_in, "group", scatter_dimension=0, tiled=True)
    grad_in = lax.all_gather(grad_in, "replica", axis=0, tiled=False)
    grad_in = jnp.sum(grad_in.astype(F32), axis=0)[:, :proj_width]
    grad_normed = dot_nt(gproj, full_in)
    unit = flat * r
    grad_gin = jnp.sum(grad_normed * unit, axis=0)
    scaled = grad_normed * gain_in
    grad_flat = r * (scaled - unit * jnp.mean(scaled * unit, axis=-1, keepdims=True))
    input_grad = (grad_flat + cot.astype(F32)).astype(BF16).reshape(tokens.shape)

    grad_skip = jnp.sum(gwide[0].reshape(heads, -1), axis=1)
    parts = [
        grad_gin, gtaps[4], gwide[1], gtaps[:4].reshape(-1),
        gheads[0, :heads], gheads[1, :heads], grad_skip,
    ]
    packed = jnp.concatenate(parts)
    packed_rows = -(-packed.shape[0] // 1024) * 8
    packed = pad_to(packed, packed_rows * LANES).reshape(packed_rows, LANES)
    packed = lax.psum(packed, ("group", "replica")).reshape(-1)
    me = lax.axis_index("group")
    xbc = gtaps.shape[1]
    starts = [0]
    for part in parts:
        starts.append(starts[-1] + part.shape[0])
    sums = [packed[starts[i] : starts[i + 1]] for i in range(len(parts))]
    return (
        layer_out,
        input_grad,
        lax.dynamic_slice_in_dim(sums[0], me * n_norm, n_norm),
        grad_in,
        lax.dynamic_slice_in_dim(sums[3].reshape(4, xbc), me * n_conv, n_conv, axis=1),
        lax.dynamic_slice_in_dim(sums[1], me * n_conv, n_conv),
        sums[4],
        sums[5],
        sums[6],
        lax.dynamic_slice_in_dim(sums[2], me * n_out, n_out),
        grad_out,
    )


def solution(mesh):
    both = P(("group", "replica"), None, None)
    in_specs = (
        both, P(("group", "replica"), None), P("group"), P("group", None), P(None, "group"),
        P("group"), P(), P(), P(), P("group"), P("group", None), both,
    )
    out_specs = (
        both, both, P("group"), P("group", None), P(None, "group"), P("group"), P(), P(), P(),
        P("group"), P("group", None),
    )
    return jax.shard_map(
        per_device, mesh=mesh, in_specs=in_specs, out_specs=out_specs, check_vma=False
    )
```

```python
import functools

import jax
import jax.numpy as jnp
from jax import lax
from jax.experimental import pallas as pl
from jax.experimental.pallas import tpu as pltpu
from jax.sharding import PartitionSpec as P

Q = 128
LANES = 128
FAR = -1e30
HIGHEST = lax.Precision.HIGHEST
F32 = jnp.float32
BF16 = jnp.bfloat16


def dot_nn(a, b, precision=None):
    return lax.dot_general(
        a, b, (((1,), (0,)), ((), ())), preferred_element_type=F32, precision=precision
    )


def dot_nt(a, b, precision=None):
    return lax.dot_general(
        a, b, (((1,), (1,)), ((), ())), preferred_element_type=F32, precision=precision
    )


def dot_tn(a, b):
    return lax.dot_general(a, b, (((0,), (0,)), ((), ())), preferred_element_type=F32)


def sigmoid(v):
    return 1.0 / (1.0 + jnp.exp(-v))


def softplus(v):
    return jnp.maximum(v, 0.0) + jnp.log(1.0 + jnp.exp(-jnp.abs(v)))


def grid_iotas():
    rows = lax.broadcasted_iota(jnp.int32, (Q, Q), 0)
    cols = lax.broadcasted_iota(jnp.int32, (Q, Q), 1)
    return rows, cols


def spread_pair(table, pair, left):
    a = jnp.broadcast_to(table[:, 2 * pair : 2 * pair + 1], (Q, LANES))
    b = jnp.broadcast_to(table[:, 2 * pair + 1 : 2 * pair + 2], (Q, LANES))
    return a, b, jnp.where(left, a, b)


def halves(v, left):
    zero = jnp.zeros_like(v)
    return jnp.concatenate([jnp.where(left, v, zero), jnp.where(left, zero, v)], axis=0)


def forward_kernel(
    inner, gates, rest, cot, segc, segr, taps, heads, wide, wout, pick,
    pre_o, state_o, cum_o, mixed_o, dgate_o, dy_o, dyy_o, gwide_o,
    state, cbuf, sbuf, conv, y_s, dmix, dyy_s,
):
    pairs = inner // LANES
    xbc = conv.shape[1]

    @pl.when(pl.program_id(1) == 0)
    def _():
        state[...] = jnp.zeros_like(state)
        cbuf[0:8, :] = jnp.zeros((8, xbc), F32)
        sbuf[0:8, :] = jnp.full((8, LANES), -1.0, F32)

    @pl.when((pl.program_id(0) == 0) & (pl.program_id(1) == 0))
    def _():
        gwide_o[...] = jnp.zeros_like(gwide_o)

    dmix[...] = dot_nt(cot[...], wout[...])
    seg = segc[...]
    sbuf[8 : 8 + Q, :] = seg
    cbuf[8 : 8 + Q, :] = rest[:, 0:xbc]
    masks = [None] + [(sbuf[8 - k : 8 - k + Q, :] == seg).astype(F32) for k in (1, 2, 3)]
    for g in range(xbc // LANES):
        cs = slice(g * LANES, (g + 1) * LANES)
        acc = taps[4:5, cs] + taps[3:4, cs] * cbuf[8 : 8 + Q, cs]
        for k in (1, 2, 3):
            acc = acc + taps[3 - k : 4 - k, cs] * (cbuf[8 - k : 8 - k + Q, cs] * masks[k])
        pre_o[:, cs] = acc
        conv[:, cs] = acc * sigmoid(acc)
    rows, cols = grid_iotas()
    left = cols < 64
    dt = softplus(rest[:, xbc : xbc + LANES] + heads[0:1, :])
    cum = dot_nn((rows >= cols).astype(F32), dt * heads[1:2, :], HIGHEST)
    cum_o[...] = cum
    cum_t = cum.T
    b_low = conv[:, inner : inner + LANES].astype(BF16)
    c_low = conv[:, inner + LANES : inner + 2 * LANES].astype(BF16)
    inter = dot_nt(c_low, b_low)
    bias = jnp.where((rows >= cols) & (seg == segr[0, 0:1, :]), 0.0, FAR)
    last_seg = sbuf[7:8, :]
    end_seg = sbuf[7 + Q : 8 + Q, :]
    carried = (seg == last_seg).astype(F32)
    tail = (seg == end_seg).astype(F32)
    keep = (end_seg == last_seg).astype(F32)
    squares = jnp.zeros((Q, LANES), F32)
    along = jnp.zeros((Q, LANES), F32)
    for p in range(pairs):
        cs = slice(p * LANES, (p + 1) * LANES)
        cum_a, cum_b, cum_p = spread_pair(cum, p, left)
        _, _, dt_p = spread_pair(dt, p, left)
        mix_a = (inter * jnp.exp(cum_a - cum_t[2 * p : 2 * p + 1, :] + bias)).astype(BF16)
        mix_b = (inter * jnp.exp(cum_b - cum_t[2 * p + 1 : 2 * p + 2, :] + bias)).astype(BF16)
        x = conv[:, cs]
        xd = (dt_p * x).astype(BF16)
        y = dot_nn(jnp.concatenate([mix_a, mix_b], axis=1), halves(xd, left))
        old = state[:, cs]
        old_low = old.astype(BF16)
        state_o[0, :, cs] = old_low
        y = y + jnp.exp(cum_p) * carried * dot_nn(c_low, old_low)
        y_s[:, cs] = y
        end = cum_p[Q - 1 : Q, :]
        xe = (jnp.exp(end - cum_p) * tail * xd.astype(F32)).astype(BF16)
        state[:, cs] = old * (jnp.exp(end) * keep) + dot_tn(b_low, xe)
        gate = gates[:, cs]
        gated = (y + wide[0:1, cs] * x) * (gate * sigmoid(gate))
        squares = squares + gated * gated
        along = along + dmix[:, cs] * wide[1:2, cs] * gated
    r = lax.rsqrt(jnp.sum(squares, axis=1, keepdims=True) / inner + 1e-5)
    lean = jnp.sum(along, axis=1, keepdims=True) / inner * r * r
    r = jnp.broadcast_to(r, (Q, LANES))
    lean = jnp.broadcast_to(lean, (Q, LANES))
    for p in range(pairs):
        cs = slice(p * LANES, (p + 1) * LANES)
        x = conv[:, cs]
        y = y_s[:, cs]
        gate = gates[:, cs]
        sg = sigmoid(gate)
        scanned = y + wide[0:1, cs] * x
        silu_gate = gate * sg
        gated = scanned * silu_gate
        scaled = gated * r
        mixed_o[:, cs] = (scaled * wide[1:2, cs]).astype(BF16)
        dm = dmix[:, cs]
        gwide_o[1:2, cs] += jnp.sum(dm * scaled, axis=0, keepdims=True)
        dgated = r * (dm * wide[1:2, cs] - gated * lean)
        dgate_o[:, cs] = (dgated * scanned * (sg * (1.0 + gate * (1.0 - sg)))).astype(BF16)
        dscan = dgated * silu_gate
        gwide_o[0:1, cs] += jnp.sum(dscan * x, axis=0, keepdims=True)
        dy = dscan.astype(BF16)
        dy_o[:, cs] = dy
        dyy_s[:, cs] = dy.astype(F32) * y
    dyy_o[...] = dot_nn(dyy_s[...], pick[...], HIGHEST)
    cbuf[0:8, :] = cbuf[Q : Q + 8, :]
    sbuf[0:8, :] = sbuf[Q : Q + 8, :]


def backward_kernel(
    inner, rest, pre, dy_i, dyy_i, state_i, cum_i, segc, segr, segp, taps, heads, wide, pick,
    gproj_o, gtaps_o, gheads_o,
    dstate, dbuf, sbuf, conv, slope, dcum_s, ddt_s, far_s, held_s,
):
    pairs = inner // LANES
    xbc = conv.shape[1]

    @pl.when(pl.program_id(1) == 0)
    def _():
        dstate[...] = jnp.zeros_like(dstate)
        dbuf[Q : Q + 8, :] = jnp.zeros((8, xbc), F32)
        sbuf[Q : Q + 8, :] = jnp.full((8, LANES), -1.0, F32)

    @pl.when((pl.program_id(0) == 0) & (pl.program_id(1) == 0))
    def _():
        gtaps_o[...] = jnp.zeros_like(gtaps_o)
        gheads_o[...] = jnp.zeros_like(gheads_o)

    seg = segc[...]
    sbuf[0:Q, :] = seg
    rows, cols = grid_iotas()
    left = cols < 64
    for g in range(xbc // LANES):
        cs = slice(g * LANES, (g + 1) * LANES)
        v = pre[:, cs]
        s = sigmoid(v)
        conv[:, cs] = v * s
        slope[:, cs] = s * (1.0 + v * (1.0 - s))
    raw = rest[:, xbc : xbc + LANES] + heads[0:1, :]
    dt = softplus(raw)
    cum = cum_i[...]
    cum_t = cum.T
    b_low = conv[:, inner : inner + LANES].astype(BF16)
    c_low = conv[:, inner + LANES : inner + 2 * LANES].astype(BF16)
    inter_t = dot_nt(b_low, c_low)
    bias_t = jnp.where((rows <= cols) & (seg == segr[0, 0:1, :]), 0.0, FAR)
    last_seg = segp[0, 0:1, :]
    end_seg = sbuf[Q - 1 : Q, :]
    carried = (seg == last_seg).astype(F32)
    tail = (seg == end_seg).astype(F32)
    keep = (end_seg == last_seg).astype(F32)
    dinter_t = jnp.zeros((Q, Q), F32)
    d_b = jnp.zeros((Q, LANES), F32)
    d_c = jnp.zeros((Q, LANES), F32)
    for p in range(pairs):
        cs = slice(p * LANES, (p + 1) * LANES)
        x = conv[:, cs]
        cum_a, cum_b, cum_p = spread_pair(cum, p, left)
        _, _, dt_p = spread_pair(dt, p, left)
        decay_a = jnp.exp(cum_t[2 * p : 2 * p + 1, :] - cum_a + bias_t)
        decay_b = jnp.exp(cum_t[2 * p + 1 : 2 * p + 2, :] - cum_b + bias_t)
        mix_a = (inter_t * decay_a).astype(BF16)
        mix_b = (inter_t * decay_b).astype(BF16)
        dy = dy_i[:, cs]
        dy_wide = dy.astype(F32)
        xd = (dt_p * x).astype(BF16)
        xd_wide = xd.astype(F32)
        end = cum_p[Q - 1 : Q, :]
        to_end = jnp.exp(end - cum_p) * tail
        dst = dstate[:, cs]
        dst_low = dst.astype(BF16)
        dxd = dot_nn(jnp.concatenate([mix_a, mix_b], axis=1), halves(dy, left))
        dxd_far = to_end * dot_nn(b_low, dst_low)
        dcum_s[:, cs] = xd_wide * dxd
        far_s[:, cs] = xd_wide * dxd_far
        dxd = dxd + dxd_far
        dmix_t = dot_nt(halves(xd, left), dy)
        dinter_t = dinter_t + dmix_t[0:Q, :] * decay_a + dmix_t[Q : 2 * Q, :] * decay_b
        edy = (jnp.exp(cum_p) * carried * dy_wide).astype(BF16)
        xe = (to_end * xd_wide).astype(BF16)
        d_b = d_b + dot_nt(xe, dst_low)
        d_c = d_c + dot_nt(edy, state_i[0, :, cs])
        kept = dst * (jnp.exp(end) * keep)
        held = jnp.sum(kept * state_i[0, :, cs].astype(F32), axis=0, keepdims=True)
        held_s[:, cs] = jnp.broadcast_to(held, (8, LANES))
        dstate[:, cs] = kept + dot_tn(c_low, edy)
        ddt_s[:, cs] = x * dxd
        dbuf[0:Q, cs] = (dy_wide * wide[0:1, cs] + dt_p * dxd) * slope[:, cs]
    d_b = d_b + dot_nn(dinter_t.astype(BF16), c_low)
    d_c = d_c + dot_nn(dinter_t.T.astype(BF16), b_low)
    bs = slice(inner, inner + LANES)
    os = slice(inner + LANES, inner + 2 * LANES)
    dbuf[0:Q, bs] = d_b * slope[:, bs]
    dbuf[0:Q, os] = d_c * slope[:, os]

    dcum = dyy_i[...] - dot_nn(dcum_s[...], pick[...], HIGHEST)
    ddt = dot_nn(ddt_s[...], pick[...], HIGHEST)
    rate = heads[1:2, :]
    far = dot_nn(far_s[...], pick[...], HIGHEST)
    held = dot_nn(held_s[...], pick[...], HIGHEST)[0:1, :]
    later = dot_nn((rows <= cols).astype(F32), dcum, HIGHEST)
    later = later + dot_nn((rows > cols).astype(F32), far, HIGHEST) + held
    gheads_o[1:2, :] += jnp.sum(later * dt * rate, axis=0, keepdims=True)
    dstep = (ddt + later * rate) * sigmoid(raw)
    gheads_o[0:1, :] += jnp.sum(dstep, axis=0, keepdims=True)
    gproj_o[:, xbc : xbc + LANES] = dstep.astype(BF16)

    masks = [None] + [(sbuf[k : k + Q, :] == seg).astype(F32) for k in (1, 2, 3)]
    for g in range(xbc // LANES):
        cs = slice(g * LANES, (g + 1) * LANES)
        here = rest[:, cs]
        now = dbuf[0:Q, cs]
        total = taps[3:4, cs] * now
        gtaps_o[4:5, cs] += jnp.sum(now, axis=0, keepdims=True)
        gtaps_o[3:4, cs] += jnp.sum(now * here, axis=0, keepdims=True)
        for k in (1, 2, 3):
            moved = dbuf[k : k + Q, cs] * masks[k]
            total = total + taps[3 - k : 4 - k, cs] * moved
            gtaps_o[3 - k : 4 - k, cs] += jnp.sum(moved * here, axis=0, keepdims=True)
        gproj_o[:, cs] = total.astype(BF16)
    dbuf[Q : Q + 8, :] = dbuf[0:8, :]
    sbuf[Q : Q + 8, :] = sbuf[0:8, :]


VMEM_LIMIT = 52 * 1024 * 1024


def mixer_tables(segments, taps, bias, step_bias, log_decay, skip_scale, gain):
    seqs, length = segments.shape
    chunks = length // Q
    heads, inner = step_bias.shape[0], gain.shape[0]
    segf = segments.astype(F32)
    segc = jnp.broadcast_to(segf.reshape(seqs * length, 1), (seqs * length, LANES))
    blocks = segf.reshape(seqs * chunks, 1, Q)
    segr = jnp.broadcast_to(blocks, (seqs * chunks, 8, Q))
    lasts = segf.reshape(seqs, chunks, Q)[:, :, Q - 1]
    before = jnp.concatenate([jnp.full((seqs, 1), -1.0, F32), lasts[:, :-1]], axis=1)
    segp = jnp.broadcast_to(before.reshape(seqs * chunks, 1, 1), (seqs * chunks, 8, LANES))
    taps8 = jnp.concatenate([taps, bias[None], jnp.zeros((3, taps.shape[1]), F32)], axis=0)
    head8 = jnp.zeros((8, LANES), F32)
    head8 = head8.at[0, :heads].set(step_bias).at[1, :heads].set(-jnp.exp(log_decay))
    wide8 = jnp.concatenate(
        [jnp.repeat(skip_scale, inner // heads)[None], gain[None], jnp.zeros((6, inner), F32)], axis=0
    )
    owner = jnp.arange(inner)[:, None] // (inner // heads)
    pick = (owner == jnp.arange(LANES)[None, :]).astype(F32)
    return segc, segr, segp, taps8, head8, wide8, pick


def mixer_forward(gates, rest, cot, wout, tables, seqs):
    segc, segr, segp, taps8, head8, wide8, pick = tables
    rows, width = rest.shape
    inner, xbc = wide8.shape[1], taps8.shape[1]
    chunks = rows // seqs // Q

    def at(s, c):
        return (s * chunks + c, 0)

    def at3(s, c):
        return (s * chunks + c, 0, 0)

    def still(s, c):
        return (0, 0)

    return pl.pallas_call(
        functools.partial(forward_kernel, inner),
        grid=(seqs, chunks),
        in_specs=[
            pl.BlockSpec((Q, inner), at),
            pl.BlockSpec((Q, width), at),
            pl.BlockSpec((Q, cot.shape[1]), at),
            pl.BlockSpec((Q, LANES), at),
            pl.BlockSpec((1, 8, Q), at3),
            pl.BlockSpec((8, xbc), still),
            pl.BlockSpec((8, LANES), still),
            pl.BlockSpec((8, inner), still),
            pl.BlockSpec(wout.shape, still),
            pl.BlockSpec((inner, LANES), still),
        ],
        out_specs=[
            pl.BlockSpec((Q, xbc), at),
            pl.BlockSpec((1, LANES, inner), at3),
            pl.BlockSpec((Q, LANES), at),
            pl.BlockSpec((Q, inner), at),
            pl.BlockSpec((Q, inner), at),
            pl.BlockSpec((Q, inner), at),
            pl.BlockSpec((Q, LANES), at),
            pl.BlockSpec((8, inner), still),
        ],
        out_shape=[
            jax.ShapeDtypeStruct((rows, xbc), F32),
            jax.ShapeDtypeStruct((seqs * chunks, LANES, inner), BF16),
            jax.ShapeDtypeStruct((rows, LANES), F32),
            jax.ShapeDtypeStruct((rows, inner), BF16),
            jax.ShapeDtypeStruct((rows, inner), BF16),
            jax.ShapeDtypeStruct((rows, inner), BF16),
            jax.ShapeDtypeStruct((rows, LANES), F32),
            jax.ShapeDtypeStruct((8, inner), F32),
        ],
        scratch_shapes=[
            pltpu.VMEM((LANES, inner), F32),
            pltpu.VMEM((Q + 8, xbc), F32),
            pltpu.VMEM((Q + 8, LANES), F32),
            pltpu.VMEM((Q, xbc), F32),
            pltpu.VMEM((Q, inner), F32),
            pltpu.VMEM((Q, inner), F32),
            pltpu.VMEM((Q, inner), F32),
        ],
        compiler_params=pltpu.CompilerParams(vmem_limit_bytes=VMEM_LIMIT),
        cost_estimate=pl.CostEstimate(flops=2 * 10**9, bytes_accessed=10**8, transcendentals=10**7),
        name="mixer_forward",
    )(gates, rest, cot, segc, segr, taps8, head8, wide8, wout, pick)


def mixer_backward(rest, pre, dy, dyy, states, cum, tables, seqs):
    segc, segr, segp, taps8, head8, wide8, pick = tables
    rows, width = rest.shape
    inner, xbc = wide8.shape[1], taps8.shape[1]
    chunks = rows // seqs // Q

    def at(s, c):
        return (s * chunks + chunks - 1 - c, 0)

    def at3(s, c):
        return (s * chunks + chunks - 1 - c, 0, 0)

    def still(s, c):
        return (0, 0)

    return pl.pallas_call(
        functools.partial(backward_kernel, inner),
        grid=(seqs, chunks),
        in_specs=[
            pl.BlockSpec((Q, width), at),
            pl.BlockSpec((Q, xbc), at),
            pl.BlockSpec((Q, inner), at),
            pl.BlockSpec((Q, LANES), at),
            pl.BlockSpec((1, LANES, inner), at3),
            pl.BlockSpec((Q, LANES), at),
            pl.BlockSpec((Q, LANES), at),
            pl.BlockSpec((1, 8, Q), at3),
            pl.BlockSpec((1, 8, LANES), at3),
            pl.BlockSpec((8, xbc), still),
            pl.BlockSpec((8, LANES), still),
            pl.BlockSpec((8, inner), still),
            pl.BlockSpec((inner, LANES), still),
        ],
        out_specs=[
            pl.BlockSpec((Q, width), at),
            pl.BlockSpec((8, xbc), still),
            pl.BlockSpec((8, LANES), still),
        ],
        out_shape=[
            jax.ShapeDtypeStruct((rows, width), BF16),
            jax.ShapeDtypeStruct((8, xbc), F32),
            jax.ShapeDtypeStruct((8, LANES), F32),
        ],
        scratch_shapes=[
            pltpu.VMEM((LANES, inner), F32),
            pltpu.VMEM((Q + 8, xbc), F32),
            pltpu.VMEM((Q + 8, LANES), F32),
            pltpu.VMEM((Q, xbc), F32),
            pltpu.VMEM((Q, xbc), F32),
            pltpu.VMEM((Q, inner), F32),
            pltpu.VMEM((Q, inner), F32),
            pltpu.VMEM((Q, inner), F32),
            pltpu.VMEM((8, inner), F32),
        ],
        compiler_params=pltpu.CompilerParams(vmem_limit_bytes=VMEM_LIMIT),
        cost_estimate=pl.CostEstimate(
            flops=5 * 10**9, bytes_accessed=2 * 10**8, transcendentals=2 * 10**7
        ),
        name="mixer_backward",
    )(rest, pre, dy, dyy, states, cum, segc, segr, segp, taps8, head8, wide8, pick)


def pad_to(v, size):
    return jnp.concatenate([v, jnp.zeros((size - v.shape[0],), v.dtype)])


def per_device(
    tokens, segments, norm_gain, in_weight, conv_weight, conv_bias, step_bias, log_decay,
    skip_scale, out_gain, out_weight, cotangent,
):
    seqs, length, model = tokens.shape
    rows = seqs * length
    heads = step_bias.shape[0]
    proj_width = in_weight.shape[1]
    full_width = -(-proj_width // LANES) * LANES
    n_norm, n_conv, n_out = norm_gain.shape[0], conv_bias.shape[0], out_gain.shape[0]

    inner = out_weight.shape[0] * lax.axis_size("group")
    in_rows, width = in_weight.shape[0], full_width - inner
    small = jnp.concatenate([norm_gain, conv_weight.reshape(-1), conv_bias, out_gain])
    n_small = small.shape[0]
    small = pad_to(small, 16 * width).reshape(16, width)
    padded = jnp.pad(in_weight[:, inner:], ((0, 0), (0, full_width - proj_width)))
    joined = lax.all_gather(jnp.concatenate([padded, small], axis=0), "group", axis=0, tiled=False)
    in_gate = lax.all_gather(in_weight[:, :inner], "group", axis=0, tiled=True)
    full_out = lax.all_gather(out_weight, "group", axis=0, tiled=True)
    in_rest = joined[:, :in_rows].reshape(-1, width)
    small = joined[:, in_rows:].reshape(-1, 16 * width)[:, :n_small].astype(F32)
    shards = small.shape[0]
    cuts = [n_norm, n_norm + 4 * n_conv, n_norm + 5 * n_conv, n_small]
    gain_in = small[:, : cuts[0]].reshape(-1)
    taps = small[:, cuts[0] : cuts[1]].reshape(shards, 4, n_conv)
    taps = taps.transpose(1, 0, 2).reshape(4, -1)
    bias = small[:, cuts[1] : cuts[2]].reshape(-1)
    gain_out = small[:, cuts[2] : cuts[3]].reshape(-1)
    tables = mixer_tables(segments, taps, bias, step_bias, log_decay, skip_scale, gain_out)

    flat = tokens.reshape(rows, model).astype(F32)
    r = lax.rsqrt(jnp.mean(flat * flat, axis=-1, keepdims=True) + 1e-05)
    normed = (flat * r * gain_in).astype(BF16)
    cot = cotangent.reshape(rows, model)
    rest = dot_nn(normed, in_rest)
    gates = dot_nn(normed, in_gate)
    pre, states, cum, mixed, dgate, dy, dyy, gwide = mixer_forward(
        gates, rest, cot, full_out, tables, seqs
    )

    def gather_sum(v):
        v = lax.all_gather(v, "replica", axis=0, tiled=False)
        return jnp.sum(v.astype(F32), axis=0)

    def scatter(v):
        return lax.psum_scatter(v.astype(BF16), "group", scatter_dimension=0, tiled=True)

    grad_gate = dot_tn(normed, dgate).astype(BF16)
    grad_out = dot_tn(mixed, cot).astype(BF16)
    dy, grad_gate, grad_out = lax.optimization_barrier((dy, grad_gate, grad_out))
    grad_gate = scatter(grad_gate)
    grad_out = scatter(grad_out)
    branch = dot_nn(mixed, full_out)
    layer_out = (flat + branch).astype(BF16).reshape(tokens.shape)
    grad_normed = dot_nt(dgate, in_gate)
    grest, gtaps, gheads = mixer_backward(rest, pre, dy, dyy, states, cum, tables, seqs)
    grest, grad_gate, grad_out = lax.optimization_barrier((grest, grad_gate, grad_out))
    grad_gate = gather_sum(grad_gate)
    grad_out = gather_sum(grad_out)
    grad_normed = grad_normed + dot_nt(grest, in_rest)
    grad_rest = dot_tn(normed, grest)
    unit = flat * r
    grad_gin = jnp.sum(grad_normed * unit, axis=0)
    scaled = grad_normed * gain_in
    grad_flat = r * (scaled - unit * jnp.mean(scaled * unit, axis=-1, keepdims=True))
    input_grad = (grad_flat + cot.astype(F32)).astype(BF16).reshape(tokens.shape)

    grad_skip = jnp.sum(gwide[0].reshape(heads, -1), axis=1)
    per_head = jnp.concatenate([gheads[0, :heads], gheads[1, :heads], grad_skip])
    split_taps = gtaps[:4].reshape(4, shards, n_conv).transpose(1, 0, 2).reshape(shards, -1)
    packed = jnp.concatenate(
        [
            grad_gin.reshape(shards, -1),
            split_taps,
            gtaps[4].reshape(shards, -1),
            gwide[1].reshape(shards, -1),
            jnp.broadcast_to(per_head[None], (shards, 3 * heads)),
        ],
        axis=1,
    )
    packed = jnp.pad(packed, ((0, 0), (0, 16 * width - packed.shape[1])))
    packed = packed.reshape(shards, 16, width)
    sent = jnp.concatenate([grad_rest.reshape(shards, in_rows, width), packed], axis=1)
    sums = gather_sum(scatter(sent.reshape(-1, width)))
    grad_in = jnp.concatenate([grad_gate, sums[:in_rows, : proj_width - inner]], axis=1)
    tail = sums[in_rows:].reshape(-1)
    ends = n_small + heads, n_small + 2 * heads, n_small + 3 * heads
    return (
        layer_out,
        input_grad,
        tail[: cuts[0]],
        grad_in,
        tail[cuts[0] : cuts[1]].reshape(4, n_conv),
        tail[cuts[1] : cuts[2]],
        tail[n_small : ends[0]],
        tail[ends[0] : ends[1]],
        tail[ends[1] : ends[2]],
        tail[cuts[2] : cuts[3]],
        grad_out,
    )


def solution(mesh):
    both = P(("group", "replica"), None, None)
    in_specs = (
        both, P(("group", "replica"), None), P("group"), P("group", None), P(None, "group"),
        P("group"), P(), P(), P(), P("group"), P("group", None), both,
    )
    out_specs = (
        both, both, P("group"), P("group", None), P(None, "group"), P("group"), P(), P(), P(),
        P("group"), P("group", None),
    )
    return jax.shard_map(
        per_device, mesh=mesh, in_specs=in_specs, out_specs=out_specs, check_vma=False
    )
```
